256 devices in a mesh: lon: 4 (over x), lat: 64 (over z, y, core).
Axes of the slice: x: 4, y: 4, z: 8, core: 2. Of those that a mesh axis runs over, the one named last changes fastest.
Arguments:
- fields: float32 [2880, 720, 96], P('lat', 'lon'), may hold values from -6 to 6
- weight_one: float32 [8, 2, 96, 96], replicated, may hold values from -0.4375 to 0.4375
- weight_two: float32 [8, 2, 96, 96], replicated, may hold values from -0.4375 to 0.4375
- gate_mask: int32 [256, 2, 8, 360, 96], P(('lon', 'lat')), may hold values 0 or 1
- shrink_mask: int32 [256, 2, 8, 360, 96], P(('lon', 'lat')), may hold values 0 or 1
Outputs:
- tangent_out: float32 [2880, 720, 96], P('lat', 'lon')
The draws below stay inside these ranges and needn't reach their ends.
All inputs are finite; a program needn't handle non-finite values. No bound on the sum of `gate_mask` or of `shrink_mask` on one device may be relied on, other than what follows from the above.
Results may differ from the reference program's by a relative error of at most 0.00007.
Values sent between devices are 32-bit elements; how exact they have to be, the bound alone decides.
A program may use at most 128 MiB of HBM per device.

```python
import jax
import jax.numpy as jnp
from jax import lax

W = 720
H = 360
C = 96
KW = 256
NB = 8


def touch_ends(entries, key, low, largest):
    longest = entries.shape.index(max(entries.shape))
    spots = []
    for shift in (0, 1):
        where = [jax.random.randint(jax.random.fold_in(key, axis), (), 0, length) for axis, length in enumerate(entries.shape)]
        where[longest] = (where[longest] + shift) % entries.shape[longest]
        spots.append(tuple(where))
    return entries.at[spots[0]].set(low).at[spots[1]].set(largest)


def levels(stream_key, dims, shards, smallest, high):
    gain, own = 1.0, jax.random.fold_in(stream_key, 6)
    for dim, parts in shards:
        heights = jnp.exp(jax.random.uniform(jax.random.fold_in(own, dim), (parts,), jnp.float32, smallest / len(shards), high / len(shards)))
        gain = gain * jnp.repeat(heights, dims[dim] // parts).reshape([-1 if axis == dim else 1 for axis in range(len(dims))])
    return gain


def scatter_about(stream_key, extent, spread, most, cuts=(), kind=jnp.bfloat16):
    drawn = spread * jax.random.normal(stream_key, extent, jnp.float32)
    if cuts:
        drawn = drawn * levels(stream_key, extent, cuts, -0.22, 0.18)
    return jnp.clip(drawn, -most, most).astype(kind)


def setup_inputs(seed: int = 0) -> dict:
    key_of = jax.random.split(jax.random.key(seed), 6)
    return {
        "fields": scatter_about(key_of[0], (NB * H, W, C), 1.0, 6.0, ((0, 64), (1, 4)), jnp.float32),
        "weight_one": scatter_about(key_of[1], (NB, 2, C, C), (2 * C) ** -0.5, 0.4375, (), jnp.float32),
        "weight_two": scatter_about(key_of[2], (NB, 2, C, C), (2 * C) ** -0.5, 0.4375, (), jnp.float32),
        "gate_mask": touch_ends((jax.random.randint(key_of[3], (KW, 2, NB, H, C), 0, 2) < 1).astype(jnp.int32), jax.random.fold_in(key_of[3], 1), 0, 1),
        "shrink_mask": touch_ends((jax.random.randint(key_of[4], (KW, 2, NB, H, C), 0, 4) < 3).astype(jnp.int32), jax.random.fold_in(key_of[4], 1), 0, 1),
    }


def complex_mix(real_part, imag_part, weights):
    highest = lax.Precision.HIGHEST
    out_real = jnp.einsum("hkc,cd->hkd", real_part, weights[0], precision=highest) - jnp.einsum("hkc,cd->hkd", imag_part, weights[1], precision=highest)
    out_imag = jnp.einsum("hkc,cd->hkd", imag_part, weights[0], precision=highest) + jnp.einsum("hkc,cd->hkd", real_part, weights[1], precision=highest)
    return out_real, out_imag


def one_block(packed):
    block, first, second, gates, shrink = packed
    along_lon = jnp.fft.rfft(block, axis=1, norm="ortho")[:, :KW]
    spectrum = jnp.fft.fft(along_lon, axis=0, norm="ortho")
    gates = gates.astype(block.dtype)
    shrink = shrink.astype(block.dtype)
    hid_real, hid_imag = complex_mix(jnp.real(spectrum), jnp.imag(spectrum), first)
    hid_real = hid_real * gates[0]
    hid_imag = hid_imag * gates[1]
    mix_real, mix_imag = complex_mix(hid_real, hid_imag, second)
    mix_real = mix_real * shrink[0]
    mix_imag = mix_imag * shrink[1]
    band = jnp.fft.ifft(mix_real + 1j * mix_imag, axis=0, norm="ortho")
    padded = jnp.pad(band, ((0, 0), (0, W // 2 + 1 - KW), (0, 0)))
    return jnp.fft.irfft(padded, n=W, axis=1, norm="ortho").astype(block.dtype)


def reference(fields, weight_one, weight_two, gate_mask, shrink_mask):
    blocks = fields.reshape(NB, H, W, C)
    gates = jnp.transpose(gate_mask, (2, 1, 3, 0, 4))
    shrink = jnp.transpose(shrink_mask, (2, 1, 3, 0, 4))
    result = lax.map(one_block, (blocks, weight_one, weight_two, gates, shrink))
    return result.reshape(NB * H, W, C)
```

```python
import functools
import math

import jax
import jax.numpy as jnp
import ml_dtypes
import numpy as np
from jax import lax
from jax.experimental import pallas as pl
from jax.experimental.pallas import tpu as pltpu
from jax.sharding import PartitionSpec as P

MESH = pl.DeviceIdType.MESH
W = 720
H = 360
C = 96
KW = 256
NB = 8
NX = 4
NS = 32
HL = 45
WL = 180
WP = 184
KP = 192
RP = 12
NG = 3
MP = 384
NT = 9
MSG = NT * 8
F32 = jnp.float32
BF16 = jnp.bfloat16


def split_table(table):
    high = table.astype(ml_dtypes.bfloat16)
    low = (table - high.astype(np.float64)).astype(ml_dtypes.bfloat16)
    return np.stack([high, low])


@functools.lru_cache(None)
def tables():
    half = np.arange(2)[:, None, None, None]
    dest = np.arange(NS)[None, :, None, None]
    part = np.arange(2)[None, None, :, None]
    four = np.arange(4)[None, None, None, :]
    mode = 64 * (dest // 8) + 8 * (4 * half + four) + dest % 8 + 0 * part
    part = part + 0 * mode
    mode, part = mode.reshape(2, 256), part.reshape(2, 256)

    def wave(angle, which):
        return np.where(which == 0, np.cos(angle), -np.sin(angle))

    depth = np.arange(NX * KP)
    lon = 180 * (depth // KP) + depth % KP
    angle = 2 * math.pi / W * (mode[:, :, None] * lon % W)
    forward = wave(angle, part[:, :, None]) / math.sqrt(W) * (depth % KP < WL)

    rows = np.arange(NX * WP)
    lon = 180 * (rows // WP) + rows % WP
    angle = 2 * math.pi / W * (mode[:, None, :] * lon[:, None] % W)
    factor = np.where(mode == 0, 1.0, 2.0)[:, None, :]
    back = wave(angle, part[:, None, :]) * factor / math.sqrt(W) * (rows % WP < WL)[:, None]

    place = np.arange(MP)
    source = place % NS
    local_row = RP * (source // 8) + place // NS
    lat = HL * (source % 8) + local_row
    m = np.arange(MP)
    angle = 2 * math.pi / H * (m[:, None] * lat[None, :] % H)
    keep = (m < H)[:, None] * (local_row < HL)[None, :] / math.sqrt(H)
    cosine, sine = np.cos(angle) * keep, np.sin(angle) * keep
    lat_fwd = np.block([[cosine, sine], [-sine, cosine]])
    lat_back = lat_fwd.T
    return tuple(split_table(t) for t in (forward, lat_fwd, lat_back, back))


def high_low(value):
    high = value.astype(BF16)
    return high, (value - high.astype(F32)).astype(BF16)


def dot3(a, b, dims=((1,), (0,))):
    def one(p, q):
        return lax.dot_general(p, q, (dims, ((), ())), preferred_element_type=F32)

    return one(a[0], b[0]) + (one(a[0], b[1]) + one(a[1], b[0]))


NT_DIMS = ((1,), (1,))


def kernel(
    fields, w1, w2, gate, shrink, t_fwd, t_lat, t_bck, t_inv, out,
    fv, xs, xr, xhi, xlo, ys, yr, cs, cr, osn, orc, ov, gv, sv, wv, wt,
    vfwd, vlat, vbck, vinv, shi, slo, phi, plo, hhi, hlo, mhi, mlo,
    s_load, s_out, sa, ra, sb, rb, sc, rc, sd, rd, sm, rm,
):
    x = lax.axis_index("lon")
    t = lax.axis_index("lat")
    z = t // 8
    yc = t % 8
    y = yc // 2
    core = yc % 2
    me = x * 8 + yc
    zh = z // 4
    zl = z % 4

    load_fields = pltpu.make_async_copy(fields, fv.at[pl.ds(0, HL)], s_load.at[0])
    load_fields.start()
    loads = [
        pltpu.make_async_copy(w1.at[z], wv.at[0], s_load.at[1]),
        pltpu.make_async_copy(w2.at[z], wv.at[1], s_load.at[2]),
        pltpu.make_async_copy(t_fwd, vfwd, s_load.at[3]),
        pltpu.make_async_copy(t_lat, vlat, s_load.at[4]),
        pltpu.make_async_copy(t_bck, vbck, s_load.at[5]),
        pltpu.make_async_copy(t_inv, vinv, s_load.at[6]),
    ]
    for copy in loads:
        copy.start()

    def plane_peer(i):
        dx, r = i % 4, i // 4
        px = (x + dx) % 4
        py = (y + r // 2 + dx) % 4
        pc = (core + r + dx) % 2
        return px * 8 + py * 2 + pc

    def plane_id(d):
        return (d // 8, z * 8 + d % 8)

    barrier = pltpu.get_barrier_semaphore()

    @pl.loop(1, NS)
    def _(i):
        pl.semaphore_signal(barrier, inc=1, device_id=plane_id(plane_peer(i)), device_id_type=MESH)

    @pl.loop(1, NB)
    def _(i):
        pl.semaphore_signal(barrier, inc=1, device_id=(x, ((z + i) % 8) * 8 + yc), device_id_type=MESH)

    fv[HL : RP * NX] = jnp.zeros((RP * NX - HL, WL, C), F32)
    hhi[...] = jnp.zeros_like(hhi)
    hlo[...] = jnp.zeros_like(hlo)
    mhi[...] = jnp.zeros_like(mhi)
    mlo[...] = jnp.zeros_like(mlo)

    def pack(g, dx, put):
        base = RP * ((x + dx) % 4) + 4 * g
        last = fv[base + 3]
        for j in range(3):
            put(j, jnp.concatenate([fv[base + j], last[:, 32 * j : 32 * j + 32]], axis=1))

    def pack_group(g):
        for dx in (2, 1, 3):

            def put(j, value):
                xs[g, dx - 1, j, WP - 8 : WP] = jnp.zeros((8, 128), F32)
                xs[g, dx - 1, j, 0:WL] = value

            pack(g, dx, put)

    def send_group(g):
        for dx in (2, 1, 3):
            pltpu.make_async_remote_copy(
                src_ref=xs.at[g, dx - 1], dst_ref=xr.at[g, x], send_sem=sa.at[g], recv_sem=ra.at[g],
                device_id=((x + dx) % 4, t), device_id_type=MESH,
            ).start()

    load_fields.wait()
    pack_group(0)
    pl.semaphore_wait(barrier, NS - 1 + NB - 1)
    send_group(0)

    def send_mask(src, dst, b, which):
        pltpu.make_async_remote_copy(
            src_ref=src.at[0, :, b], dst_ref=dst.at[z], send_sem=sm, recv_sem=rm.at[which],
            device_id=(x, b * 8 + yc), device_id_type=MESH,
        ).start()

    pltpu.make_async_copy(gate.at[0, :, z], gv.at[z], rm.at[0]).start()
    pltpu.make_async_copy(shrink.at[0, :, z], sv.at[z], rm.at[0]).start()
    for i in range(1, 4):
        send_mask(gate, gv, 4 * zh + (zl + i) % 4, 0)
        send_mask(shrink, sv, 4 * zh + (zl + i) % 4, 0)
    for i in range(4):
        send_mask(gate, gv, 4 * (1 - zh) + (zl + i) % 4, 1)
    for i in range(4):
        send_mask(shrink, sv, 4 * (1 - zh) + (zl + i) % 4, 2)

    for g in range(1, NG):
        pack_group(g)
        send_group(g)

    for g in range(NG):

        def put(j, value):
            xr[g, x, j, WP - 8 : WP] = jnp.zeros((8, 128), F32)
            xr[g, x, j, 0:WL] = value

        pack(g, 0, put)

    for copy in loads:
        copy.wait()
    for which in range(2):
        wt[...] = jnp.zeros((256, 256), F32)
        wt[0:C, 0:C] = wv[which, 0]
        wt[0:C, 128 : 128 + C] = wv[which, 1]
        wt[128 : 128 + C, 0:C] = -wv[which, 1]
        wt[128 : 128 + C, 128 : 128 + C] = wv[which, 0]
        turned = wt[...].T
        high, low = high_low(turned)
        if which == 0:
            w1t = (high, low)
        else:
            w2t = (high, low)

    for g in range(NG):
        pltpu.make_async_copy(xr.at[g, pl.ds(0, 3)], xr.at[g, pl.ds(0, 3)], ra.at[g]).wait()
        for s in range(NX):
            for j in range(3):
                value = jnp.concatenate([xr[g, s, j], jnp.zeros((KP - WP, 128), F32)], axis=0)
                high, low = high_low(value)
                xhi[KP * s : KP * s + KP, 128 * j : 128 * j + 128] = high
                xlo[KP * s : KP * s + KP, 128 * j : 128 * j + 128] = low
        for turn in range(2):
            half = (zh + turn) % 2
            modes = dot3((vfwd[0, half], vfwd[1, half]), (xhi[...], xlo[...]))
            for j in range(3):
                tile = 8 * (3 * g + j)
                ys[half, :, tile : tile + 8, :] = modes[:, 128 * j : 128 * j + 128].reshape(NS, 8, 128)
            if g == NG - 1:
                own = pltpu.make_async_copy(ys.at[half, me], yr.at[half, me], rb.at[half])
                own.start()

                @pl.loop(1, NS)
                def _(i):
                    d = plane_peer(i)
                    pltpu.make_async_remote_copy(
                        src_ref=ys.at[half, d], dst_ref=yr.at[half, me], send_sem=sb.at[half], recv_sem=rb.at[half],
                        device_id=plane_id(d), device_id_type=MESH,
                    ).start()

    yflat = yr.reshape(2, NS * MSG, 128)
    cflat = cs.reshape(2, NS * MSG, 128)
    for turn in range(2):
        half = (zh + turn) % 2
        pltpu.make_async_copy(yr.at[half], yr.at[half], rb.at[half]).wait()
        if turn == 0:
            pltpu.make_async_copy(gv, gv, rm.at[0]).wait()
        else:
            pltpu.make_async_copy(gv.at[pl.ds(0, 4)], gv.at[pl.ds(0, 4)], rm.at[1]).wait()
            pltpu.make_async_copy(sv.at[pl.ds(0, 4)], sv.at[pl.ds(0, 4)], rm.at[2]).wait()

        @pl.loop(0, 2)
        def _(pair):
            for pos in range(2):
                for ri in range(2):
                    for g in range(NG):
                        tiles = [
                            yflat[half, pl.ds((3 * g + j) * 8 + ri * 4 + 2 * pair + pos, NS, stride=MSG), :]
                            for j in range(3)
                        ]
                        last = jnp.concatenate([v[:, C:] for v in tiles] + [tiles[0][:, C:]], axis=1)
                        for r, value in enumerate(tiles + [last]):
                            high, low = high_low(value)
                            at = ri * MP + (g * 4 + r) * NS
                            shi[at : at + NS, 128 * pos : 128 * pos + 128] = high
                            slo[at : at + NS, 128 * pos : 128 * pos + 128] = low
            spec = dot3((vlat[0], vlat[1]), (shi[...], slo[...]))
            for pos in range(2):
                for ri in range(2):
                    high, low = high_low(spec[MP * ri : MP * ri + MP, 128 * pos : 128 * pos + 128])
                    phi[pos, :, 128 * ri : 128 * ri + 128] = high
                    plo[pos, :, 128 * ri : 128 * ri + 128] = low
            for pos in range(2):
                q = 4 * half + 2 * pair + pos
                hid = dot3(w1t, (phi[pos], plo[pos]), NT_DIMS)
                for ri in range(2):
                    high, low = high_low(hid[128 * ri : 128 * ri + C, 0:H] * gv[q, ri].astype(F32))
                    hhi[128 * ri : 128 * ri + C, 0:H] = high
                    hlo[128 * ri : 128 * ri + C, 0:H] = low
                mix = dot3(w2t, (hhi[...], hlo[...]))
                for ri in range(2):
                    high, low = high_low(mix[128 * ri : 128 * ri + C, 0:H] * sv[q, ri].astype(F32))
                    mhi[128 * pos : 128 * pos + C, MP * ri : MP * ri + H] = high
                    mlo[128 * pos : 128 * pos + C, MP * ri : MP * ri + H] = low
            band = dot3((vbck[0], vbck[1]), (mhi[...], mlo[...]), NT_DIMS)
            for pos in range(2):
                for ri in range(2):
                    for g in range(NG):
                        at = ri * MP + g * 4 * NS
                        rows = [
                            band[at + r * NS : at + r * NS + NS, 128 * pos : 128 * pos + 128] for r in range(4)
                        ]
                        for j in range(3):
                            value = jnp.concatenate([rows[j][:, 0:C], rows[3][:, 32 * j : 32 * j + 32]], axis=1)
                            start = (3 * g + j) * 8 + ri * 4 + 2 * pair + pos
                            cflat[half, pl.ds(start, NS, stride=MSG), :] = value

        pltpu.make_async_copy(cs.at[half, me], cr.at[half, me], rc.at[half]).start()

        @pl.loop(1, NS)
        def _(i):
            d = plane_peer(i)
            pltpu.make_async_remote_copy(
                src_ref=cs.at[half, d], dst_ref=cr.at[half, me], send_sem=sc.at[half], recv_sem=rc.at[half],
                device_id=plane_id(d), device_id_type=MESH,
            ).start()

    for half in range(2):
        pltpu.make_async_copy(cr.at[half], cr.at[half], rc.at[half]).wait()
    for g in range(NG):
        for j in range(3):
            tile = 8 * (3 * g + j)
            for half in range(2):
                high, low = high_low(cr[half, :, tile : tile + 8, :].reshape(256, 128))
                xhi[256 * half : 256 * half + 256, 128 * j : 128 * j + 128] = high
                xlo[256 * half : 256 * half + 256, 128 * j : 128 * j + 128] = low
        whole = None
        for half in range(2):
            rows = slice(256 * half, 256 * half + 256)
            term = dot3((vinv[0, half], vinv[1, half]), (xhi[rows], xlo[rows]))
            whole = term if whole is None else whole + term
        for s in range(NX):
            for j in range(3):
                osn[g, s, j] = whole[WP * s : WP * s + WP, 128 * j : 128 * j + 128]
        pltpu.make_async_copy(osn.at[g, x], orc.at[g, x], rd.at[g]).start()
        for dx in (2, 1, 3):
            to = (x + dx) % 4
            pltpu.make_async_remote_copy(
                src_ref=osn.at[g, to], dst_ref=orc.at[g, x], send_sem=sd.at[g], recv_sem=rd.at[g],
                device_id=(to, t), device_id_type=MESH,
            ).start()

    stores = []
    for g in range(NG):
        pltpu.make_async_copy(orc.at[g], orc.at[g], rd.at[g]).wait()
        for s in range(NX):
            tiles = [orc[g, s, j] for j in range(3)]
            base = RP * s + 4 * g
            count = min(4, HL - base)
            for r in range(min(3, count)):
                ov[base + r] = tiles[r][0:WL, 0:C]
            if count == 4:
                ov[base + 3] = jnp.concatenate([v[0:WL, C:] for v in tiles], axis=1)
            copy = pltpu.make_async_copy(ov.at[pl.ds(base, count)], out.at[pl.ds(base, count)], s_out.at[g, s])
            copy.start()
            stores.append(copy)

    for copy in stores:
        copy.wait()
    for g in range(NG):
        pltpu.make_async_copy(xs.at[g], xs.at[g], sa.at[g]).wait()
        pltpu.make_async_copy(xs.at[g], xs.at[g], sd.at[g]).wait()
    for half in range(2):
        sent = ys.at[half, pl.ds(0, NS - 1)]
        pltpu.make_async_copy(sent, sent, sb.at[half]).wait()
        pltpu.make_async_copy(sent, sent, sc.at[half]).wait()
    pltpu.make_async_copy(gv.at[pl.ds(0, 7)], gv.at[pl.ds(0, 7)], sm).wait()
    pltpu.make_async_copy(gv.at[pl.ds(0, 7)], gv.at[pl.ds(0, 7)], sm).wait()


def local(fields, weight_one, weight_two, gate_mask, shrink_mask):
    gate = jnp.swapaxes(gate_mask, 3, 4)
    shrink = jnp.swapaxes(shrink_mask, 3, 4)
    consts = [jnp.asarray(t) for t in tables()]
    dma = pltpu.SemaphoreType.DMA
    any_spec = pl.BlockSpec(memory_space=pl.ANY)
    vm = pltpu.VMEM
    scratch = [
        vm((RP * NX, WL, C), F32),
        vm((NG, 3, 3, WP, 128), F32),
        vm((NG, NX, 3, WP, 128), F32),
        vm((NX * KP, 384), BF16),
        vm((NX * KP, 384), BF16),
        vm((2, NS, MSG, 128), F32),
        vm((2, NS, MSG, 128), F32),
        vm((2, NS, MSG, 128), F32),
        vm((2, NS, MSG, 128), F32),
        vm((NG, NX, 3, WP, 128), F32),
        vm((NG, NX, 3, WP, 128), F32),
        vm((HL, WL, C), F32),
        vm((NB, 2, C, H), jnp.int32),
        vm((NB, 2, C, H), jnp.int32),
        vm((2, 2, C, C), F32),
        vm((256, 256), F32),
        vm((2, 2, 256, NX * KP), BF16),
        vm((2, 2 * MP, 2 * MP), BF16),
        vm((2, 2 * MP, 2 * MP), BF16),
        vm((2, 2, NX * WP, 256), BF16),
        vm((2 * MP, 256), BF16),
        vm((2 * MP, 256), BF16),
        vm((2, MP, 256), BF16),
        vm((2, MP, 256), BF16),
        vm((256, MP), BF16),
        vm((256, MP), BF16),
        vm((256, 2 * MP), BF16),
        vm((256, 2 * MP), BF16),
        dma((7,)),
        dma((NG, NX)),
        dma((NG,)),
        dma((NG,)),
        dma((2,)),
        dma((2,)),
        dma((2,)),
        dma((2,)),
        dma((NG,)),
        dma((NG,)),
        dma,
        dma((3,)),
    ]
    return pl.pallas_call(
        kernel,
        name="afno_tangent",
        out_shape=jax.ShapeDtypeStruct((HL, WL, C), F32),
        in_specs=[any_spec] * 9,
        out_specs=any_spec,
        scratch_shapes=scratch,
        compiler_params=pltpu.CompilerParams(
            collective_id=0, has_side_effects=True, vmem_limit_bytes=62 * 2**20
        ),
    )(fields, weight_one, weight_two, gate, shrink, *consts)


def solution(mesh):
    in_specs = (
        P("lat", "lon", None),
        P(),
        P(),
        P(("lon", "lat"), None, None, None, None),
        P(("lon", "lat"), None, None, None, None),
    )
    out_specs = P("lat", "lon", None)
    return jax.shard_map(local, mesh=mesh, in_specs=in_specs, out_specs=out_specs, check_vma=False)
```

```python
import functools
import math

import jax
import jax.numpy as jnp
import ml_dtypes
import numpy as np
from jax import lax
from jax.experimental import pallas as pl
from jax.experimental.pallas import tpu as pltpu
from jax.sharding import PartitionSpec as P

MESH = pl.DeviceIdType.MESH
STEPS = (0, 1, 7, 2, 6, 3, 5, 4)
W = 720
H = 360
C = 96
KW = 256
NB = 8
NX = 4
NS = 32
HL = 45
WL = 180
WP = 184
KP = 192
RP = 12
NG = 3
MP = 384
NT = 9
MSG = NT * 8
MSG2 = 40
F32 = jnp.float32
BF16 = jnp.bfloat16


def split_table(table):
    high = table.astype(ml_dtypes.bfloat16)
    low = (table - high.astype(np.float64)).astype(ml_dtypes.bfloat16)
    return np.stack([high, low])


@functools.lru_cache(None)
def tables():
    depth_z = np.arange(NB)[:, None, None]
    part = np.arange(2)[None, :, None]
    dest = np.arange(NS)[None, None, :]
    mode = 64 * (dest // 8) + 8 * depth_z + dest % 8 + 0 * part
    part = part + 0 * mode
    mode, part = mode.reshape(NB, 64), part.reshape(NB, 64)

    def wave(angle, which):
        return np.where(which == 0, np.cos(angle), -np.sin(angle))

    depth = np.arange(NX * KP)
    lon = 180 * (depth // KP) + depth % KP
    angle = 2 * math.pi / W * (mode[:, :, None] * lon % W)
    forward = wave(angle, part[:, :, None]) / math.sqrt(W) * (depth % KP < WL)

    rows = np.arange(NX * WP)
    lon = 180 * (rows // WP) + rows % WP
    angle = 2 * math.pi / W * (mode[:, None, :] * lon[:, None] % W)
    factor = np.where(mode == 0, 1.0, 2.0)[:, None, :]
    back = wave(angle, part[:, None, :]) * factor / math.sqrt(W) * (rows % WP < WL)[:, None]

    place = np.arange(MP)
    source = place % NS
    local_row = RP * (source // 8) + place // NS
    lat = HL * (source % 8) + local_row
    m = np.arange(MP)
    angle = 2 * math.pi / H * (m[:, None] * lat[None, :] % H)
    keep = (m < H)[:, None] * (local_row < HL)[None, :] / math.sqrt(H)
    cosine, sine = np.cos(angle) * keep, np.sin(angle) * keep
    lat_fwd = np.block([[cosine, sine], [-sine, cosine]])
    lat_back = lat_fwd.T
    order = (np.arange(NB)[:, None] + np.array(STEPS)[None, :]) % NB
    back = back[order].reshape(NB, 4, 2, NX * WP, 64).transpose(0, 1, 3, 2, 4).reshape(NB, 4, NX * WP, 128)
    return tuple(split_table(t) for t in (forward, lat_fwd, lat_back, back))


def high_low(value):
    high = value.astype(BF16)
    return high, (value - high.astype(F32)).astype(BF16)


def dot3(a, b, dims=((1,), (0,))):
    def one(p, q):
        return lax.dot_general(p, q, (dims, ((), ())), preferred_element_type=F32)

    return one(a[0], b[0]) + (one(a[0], b[1]) + one(a[1], b[0]))


NT_DIMS = ((1,), (1,))


def kernel(
    fields, w1, w2, gate, shrink, t_fwd, t_lat, t_bck, t_inv, out,
    fv, xs, xr, xhi, xlo, ys, yr, cs0, cr0, cs1, cr1, osn, gl, sl, gv, sv, wv, wt,
    vfwd, vlat, vbck, vinv, shi, slo, phi, plo, hhi, hlo, mhi, mlo,
    s_load, sf, sa, ra, sb, rb, sc, rc, sd, rd, sm, rm,
):
    x = lax.axis_index("lon")
    t = lax.axis_index("lat")
    z = t // 8
    yc = t % 8
    y = yc // 2
    core = yc % 2
    me = x * 8 + yc

    def field_copies(g):
        copies = []
        for s in range(NX):
            base = RP * s + 4 * g
            rows = pl.ds(base, min(4, HL - base))
            copies.append(pltpu.make_async_copy(fields.at[rows], fv.at[rows], sf.at[g, s]))
        return copies

    stages = [
        pltpu.make_async_copy(gate.at[0], gl, s_load.at[6]),
        pltpu.make_async_copy(shrink.at[0], sl, s_load.at[7]),
    ]
    for copy in stages:
        copy.start()
    for g in range(NG):
        for copy in field_copies(g):
            copy.start()
    loads = [
        pltpu.make_async_copy(w1.at[z], wv.at[0], s_load.at[0]),
        pltpu.make_async_copy(w2.at[z], wv.at[1], s_load.at[1]),
        pltpu.make_async_copy(t_fwd, vfwd, s_load.at[2]),
        pltpu.make_async_copy(t_lat, vlat, s_load.at[3]),
        pltpu.make_async_copy(t_bck, vbck, s_load.at[4]),
        pltpu.make_async_copy(t_inv.at[:, z], vinv, s_load.at[5]),
    ]
    def plane_peer(i):
        dx, r = i % 4, i // 4
        px = (x + dx) % 4
        py = (y + r // 2 + dx) % 4
        pc = (core + r + dx) % 2
        return px * 8 + py * 2 + pc

    def plane_id(d):
        return (d // 8, z * 8 + d % 8)

    barrier = pltpu.get_barrier_semaphore()

    @pl.loop(1, NS)
    def _(i):
        pl.semaphore_signal(barrier, inc=1, device_id=plane_id(plane_peer(i)), device_id_type=MESH)

    @pl.loop(1, NB)
    def _(i):
        pl.semaphore_signal(barrier, inc=1, device_id=(x, ((z + i) % 8) * 8 + yc), device_id_type=MESH)

    def pack(g, dx, put):
        base = RP * ((x + dx) % 4) + 4 * g
        last = fv[base + 3]
        for j in range(3):
            put(j, jnp.concatenate([fv[base + j], last[:, 32 * j : 32 * j + 32]], axis=1))

    def pack_group(g):
        for dx in (2, 1, 3):

            def put(j, value):
                xs[g, dx - 1, j, WP - 8 : WP] = jnp.zeros((8, 128), F32)
                xs[g, dx - 1, j, 0:WL] = value

            pack(g, dx, put)

    def send_group(g):
        for dx in (2, 1, 3):
            pltpu.make_async_remote_copy(
                src_ref=xs.at[g, dx - 1], dst_ref=xr.at[g, x], send_sem=sa.at[g], recv_sem=ra.at[g],
                device_id=((x + dx) % 4, t), device_id_type=MESH,
            ).start()

    def send_mask(src, dst, b, which):
        pltpu.make_async_remote_copy(
            src_ref=src.at[:, b], dst_ref=dst.at[z], send_sem=sm, recv_sem=rm.at[which],
            device_id=(x, b * 8 + yc), device_id_type=MESH,
        ).start()

    for copy in stages:
        copy.wait()
    pl.semaphore_wait(barrier, NS - 1 + NB - 1)
    for step, which in ((1, 0), (7, 0), (2, 0), (6, 1), (3, 1)):
        send_mask(gl, gv, (z + NB - step) % NB, which)
        send_mask(sl, sv, (z + NB - step) % NB, which)
    for src, dst, which in ((gl, gv, 2), (sl, sv, 3)):
        for step in (5, 4):
            send_mask(src, dst, (z + NB - step) % NB, which)
    pltpu.make_async_copy(gate.at[0, :, z], gv.at[z], rm.at[0]).start()
    pltpu.make_async_copy(shrink.at[0, :, z], sv.at[z], rm.at[0]).start()

    for copy in field_copies(0):
        copy.wait()
    pack_group(0)
    send_group(0)
    for copy in loads:
        copy.start()
    fv[HL : RP * NX] = jnp.zeros((RP * NX - HL, WL, C), F32)

    for g in range(1, NG):
        for copy in field_copies(g):
            copy.wait()
        pack_group(g)
        send_group(g)

    for g in range(NG):

        def put(j, value):
            xr[g, x, j, WP - 8 : WP] = jnp.zeros((8, 128), F32)
            xr[g, x, j, 0:WL] = value

        pack(g, 0, put)

    hhi[...] = jnp.zeros_like(hhi)
    hlo[...] = jnp.zeros_like(hlo)
    mhi[...] = jnp.zeros_like(mhi)
    mlo[...] = jnp.zeros_like(mlo)
    cs1[:, :, 36:40, :] = jnp.zeros((2, NS, 4, 128), F32)

    for copy in loads:
        copy.wait()
    for which in range(2):
        wt[...] = jnp.zeros((256, 256), F32)
        wt[0:C, 0:C] = wv[which, 0]
        wt[0:C, 128 : 128 + C] = wv[which, 1]
        wt[128 : 128 + C, 0:C] = -wv[which, 1]
        wt[128 : 128 + C, 128 : 128 + C] = wv[which, 0]
        turned = wt[...].T
        high, low = high_low(turned)
        if which == 0:
            w1t = (high, low)
        else:
            w2t = (high, low)

    def mode_at(u):
        return (z + STEPS[u]) % NB

    ysflat = ys.reshape(2, NS * MSG, 128)
    for g in range(NG):
        pltpu.make_async_copy(xr.at[g, pl.ds(0, 3)], xr.at[g, pl.ds(0, 3)], ra.at[g]).wait()
        for s in range(NX):
            for j in range(3):
                value = jnp.concatenate([xr[g, s, j], jnp.zeros((KP - WP, 128), F32)], axis=0)
                high, low = high_low(value)
                xhi[KP * s : KP * s + KP, 128 * j : 128 * j + 128] = high
                xlo[KP * s : KP * s + KP, 128 * j : 128 * j + 128] = low
        for half in range(2):
            table = [jnp.concatenate([vfwd[k, mode_at(4 * half + u)] for u in range(4)], axis=0) for k in range(2)]
            modes = dot3(table, (xhi[...], xlo[...]))
            for u in range(4):
                for ri in range(2):
                    for j in range(3):
                        start = (3 * g + j) * 8 + ri * 4 + u
                        ysflat[half, pl.ds(start, NS, stride=MSG), :] = modes[
                            64 * u + 32 * ri : 64 * u + 32 * ri + 32, 128 * j : 128 * j + 128
                        ]
            if g == NG - 1:
                own = pltpu.make_async_copy(ys.at[half, me], yr.at[half, me], rb.at[half])
                own.start()

                @pl.loop(1, NS)
                def _(i):
                    d = plane_peer(i)
                    pltpu.make_async_remote_copy(
                        src_ref=ys.at[half, d], dst_ref=yr.at[half, me], send_sem=sb.at[half], recv_sem=rb.at[half],
                        device_id=plane_id(d), device_id_type=MESH,
                    ).start()

    yflat = yr.reshape(2, NS * MSG, 128)
    cs0flat = cs0.reshape(NS * MSG, 128)
    cs1flat = cs1.reshape(2, NS * MSG2, 128)
    cr0flat = cr0.reshape(NS * MSG, 128)
    cr1flat = cr1.reshape(2, NS * MSG2, 128)

    def lat_forward(half, slot):
        for pos in range(2):
            for ri in range(2):
                for g in range(NG):
                    tiles = [
                        yflat[half, pl.ds((3 * g + j) * 8 + ri * 4 + 2 * slot + pos, NS, stride=MSG), :]
                        for j in range(3)
                    ]
                    last = jnp.concatenate([v[:, C:] for v in tiles] + [tiles[0][:, C:]], axis=1)
                    for r, value in enumerate(tiles + [last]):
                        high, low = high_low(value)
                        at = ri * MP + (g * 4 + r) * NS
                        shi[at : at + NS, 128 * pos : 128 * pos + 128] = high
                        slo[at : at + NS, 128 * pos : 128 * pos + 128] = low
        spec = dot3((vlat[0], vlat[1]), (shi[...], slo[...]))
        for pos in range(2):
            for ri in range(2):
                high, low = high_low(spec[MP * ri : MP * ri + MP, 128 * pos : 128 * pos + 128])
                phi[pos, :, 128 * ri : 128 * ri + 128] = high
                plo[pos, :, 128 * ri : 128 * ri + 128] = low

    def lat_back(modes, put, ready=None):
        for pos, q in enumerate(modes):
            hid = dot3(w1t, (phi[pos], plo[pos]), NT_DIMS)
            for ri in range(2):
                high, low = high_low(hid[128 * ri : 128 * ri + C, 0:H] * gv[q, ri].astype(F32))
                hhi[128 * ri : 128 * ri + C, 0:H] = high
                hlo[128 * ri : 128 * ri + C, 0:H] = low
            mix = dot3(w2t, (hhi[...], hlo[...]))
            if ready is not None and pos == 0:
                ready()
            for ri in range(2):
                high, low = high_low(mix[128 * ri : 128 * ri + C, 0:H] * sv[q, ri].astype(F32))
                mhi[128 * pos : 128 * pos + C, MP * ri : MP * ri + H] = high
                mlo[128 * pos : 128 * pos + C, MP * ri : MP * ri + H] = low
        band = dot3((vbck[0], vbck[1]), (mhi[...], mlo[...]), NT_DIMS)
        for pos in range(2):
            for ri in range(2):
                for g in range(NG):
                    at = ri * MP + g * 4 * NS
                    rows = [band[at + r * NS : at + r * NS + NS, 128 * pos : 128 * pos + 128] for r in range(4)]
                    for j in range(3):
                        value = jnp.concatenate([rows[j][:, 0:C], rows[3][:, 32 * j : 32 * j + 32]], axis=1)
                        put(3 * g + j, ri, pos, value)

    def send_back(src, dst, which):
        pltpu.make_async_copy(src.at[me], dst.at[me], rc.at[which]).start()

        @pl.loop(1, NS)
        def _(i):
            d = plane_peer(i)
            pltpu.make_async_remote_copy(
                src_ref=src.at[d], dst_ref=dst.at[me], send_sem=sc.at[which], recv_sem=rc.at[which],
                device_id=plane_id(d), device_id_type=MESH,
            ).start()

    def lat_single(i, ready=None):
        slot = i - 2

        def put(tile, ri, pos, value):
            cs1flat[slot, pl.ds(tile * 4 + ri * 2 + pos, NS, stride=MSG2), :] = value

        lat_back((mode_at(2 * i), mode_at(2 * i + 1)), put, ready)
        send_back(cs1.at[slot], cr1.at[slot], 1 + slot)

    def inverse_term(g, units, rows, pairs):
        for u in range(units):
            for ri in range(2):
                for j in range(3):
                    high, low = high_low(rows(3 * g + j, ri, u))
                    at = 64 * u + 32 * ri
                    xhi[at : at + 32, 128 * j : 128 * j + 128] = high
                    xlo[at : at + 32, 128 * j : 128 * j + 128] = low
        table = [jnp.concatenate([vinv[k, i] for i in pairs], axis=1) for k in range(2)]
        return dot3(table, (xhi[0 : 64 * units], xlo[0 : 64 * units]))

    def rows_first(tile, ri, u):
        return cr0flat[pl.ds(tile * 8 + ri * 4 + u, NS, stride=MSG), :]

    def rows_single(slot):
        return lambda tile, ri, u: cr1flat[slot, pl.ds(tile * 4 + ri * 2 + u, NS, stride=MSG2), :]

    pltpu.make_async_copy(yr.at[0], yr.at[0], rb.at[0]).wait()
    pltpu.make_async_copy(gv, gv, rm.at[0]).wait()

    @pl.loop(0, 2)
    def _(slot):
        def put(tile, ri, pos, value):
            cs0flat[pl.ds(tile * 8 + ri * 4 + 2 * slot + pos, NS, stride=MSG), :] = value

        lat_forward(0, slot)
        lat_back(((z + 7 * slot) % NB, (z + 1 + slot) % NB), put)

    send_back(cs0, cr0, 0)

    pltpu.make_async_copy(yr.at[1], yr.at[1], rb.at[1]).wait()
    pltpu.make_async_copy(gv.at[pl.ds(0, 4)], gv.at[pl.ds(0, 4)], rm.at[1]).wait()
    lat_forward(1, 0)
    lat_single(2)
    lat_forward(1, 1)

    pltpu.make_async_copy(cr0, cr0, rc.at[0]).wait()
    for g in range(NG):
        term = inverse_term(g, 4, rows_first, (0, 1))
        for s in range(NX):
            for j in range(3):
                osn[g, s, j] = term[WP * s : WP * s + WP, 128 * j : 128 * j + 128]

    def add_single(slot, g):
        term = inverse_term(g, 2, rows_single(slot), (2 + slot,))
        for s in range(NX):
            for j in range(3):
                osn[g, s, j] += term[WP * s : WP * s + WP, 128 * j : 128 * j + 128]

    pltpu.make_async_copy(cr1.at[0], cr1.at[0], rc.at[1]).wait()
    for g in range(NG):
        add_single(0, g)

    pltpu.make_async_copy(gv.at[pl.ds(0, 2)], gv.at[pl.ds(0, 2)], rm.at[2]).wait()
    lat_single(3, lambda: pltpu.make_async_copy(sv.at[pl.ds(0, 2)], sv.at[pl.ds(0, 2)], rm.at[3]).wait())

    pltpu.make_async_copy(cr1.at[1], cr1.at[1], rc.at[2]).wait()
    for g in range(NG):
        add_single(1, g)
        pltpu.make_async_copy(osn.at[g, x], out.at[g, x], rd.at[g]).start()
        for dx in (2, 1, 3):
            to = (x + dx) % 4
            pltpu.make_async_remote_copy(
                src_ref=osn.at[g, to], dst_ref=out.at[g, x], send_sem=sd.at[g], recv_sem=rd.at[g],
                device_id=(to, t), device_id_type=MESH,
            ).start()

    for g in range(NG):
        pltpu.make_async_copy(osn.at[g], osn.at[g], rd.at[g]).wait()
    for g in range(NG):
        pltpu.make_async_copy(xs.at[g], xs.at[g], sa.at[g]).wait()
        pltpu.make_async_copy(xs.at[g], xs.at[g], sd.at[g]).wait()
    for half in range(2):
        sent = ys.at[half, pl.ds(0, NS - 1)]
        pltpu.make_async_copy(sent, sent, sb.at[half]).wait()
        sent = cs1.at[half, pl.ds(0, NS - 1)]
        pltpu.make_async_copy(sent, sent, sc.at[1 + half]).wait()
    sent = cs0.at[pl.ds(0, NS - 1)]
    pltpu.make_async_copy(sent, sent, sc.at[0]).wait()
    pltpu.make_async_copy(gv.at[pl.ds(0, 7)], gv.at[pl.ds(0, 7)], sm).wait()
    pltpu.make_async_copy(gv.at[pl.ds(0, 7)], gv.at[pl.ds(0, 7)], sm).wait()


def unpack(packed, out, tiles, rows, s_in, s_out):
    def load(g, s):
        return pltpu.make_async_copy(packed.at[g, s], tiles.at[g, s], s_in.at[g, s])

    def store(g, s):
        base = RP * s + 4 * g
        span = pl.ds(base, min(4, HL - base))
        return pltpu.make_async_copy(rows.at[span], out.at[span], s_out.at[g, s])

    order = [(g, s) for s in range(NX) for g in range(NG)]
    for g, s in order:
        load(g, s).start()
    for g, s in order:
        load(g, s).wait()
        base = RP * s + 4 * g
        count = min(4, HL - base)
        for r in range(min(3, count)):
            rows[base + r] = tiles[g, s, r, 0:WL, 0:C]
        if count == 4:
            rows[base + 3] = jnp.concatenate([tiles[g, s, r, 0:WL, C:] for r in range(3)], axis=1)
        store(g, s).start()
    for g, s in order:
        store(g, s).wait()


def local(fields, weight_one, weight_two, gate_mask, shrink_mask):
    gate = jnp.swapaxes(gate_mask, 3, 4)
    shrink = jnp.swapaxes(shrink_mask, 3, 4)
    consts = [jnp.asarray(t) for t in tables()]
    dma = pltpu.SemaphoreType.DMA
    any_spec = pl.BlockSpec(memory_space=pl.ANY)
    vm = pltpu.VMEM
    scratch = [
        vm((RP * NX, WL, C), F32),
        vm((NG, 3, 3, WP, 128), F32),
        vm((NG, NX, 3, WP, 128), F32),
        vm((NX * KP, 384), BF16),
        vm((NX * KP, 384), BF16),
        vm((2, NS, MSG, 128), F32),
        vm((2, NS, MSG, 128), F32),
        vm((NS, MSG, 128), F32),
        vm((NS, MSG, 128), F32),
        vm((2, NS, MSG2, 128), F32),
        vm((2, NS, MSG2, 128), F32),
        vm((NG, NX, 3, WP, 128), F32),
        vm((2, NB, C, H), jnp.int32),
        vm((2, NB, C, H), jnp.int32),
        vm((NB, 2, C, H), jnp.int32),
        vm((NB, 2, C, H), jnp.int32),
        vm((2, 2, C, C), F32),
        vm((256, 256), F32),
        vm((2, NB, 64, NX * KP), BF16),
        vm((2, 2 * MP, 2 * MP), BF16),
        vm((2, 2 * MP, 2 * MP), BF16),
        vm((2, 4, NX * WP, 128), BF16),
        vm((2 * MP, 256), BF16),
        vm((2 * MP, 256), BF16),
        vm((2, MP, 256), BF16),
        vm((2, MP, 256), BF16),
        vm((256, MP), BF16),
        vm((256, MP), BF16),
        vm((256, 2 * MP), BF16),
        vm((256, 2 * MP), BF16),
        dma((8,)),
        dma((NG, NX)),
        dma((NG,)),
        dma((NG,)),
        dma((2,)),
        dma((2,)),
        dma((3,)),
        dma((3,)),
        dma((NG,)),
        dma((NG,)),
        dma,
        dma((4,)),
    ]
    packed = pl.pallas_call(
        kernel,
        name="afno_tangent",
        out_shape=jax.ShapeDtypeStruct((NG, NX, 3, WP, 128), F32),
        in_specs=[any_spec] * 9,
        out_specs=any_spec,
        scratch_shapes=scratch,
        compiler_params=pltpu.CompilerParams(
            collective_id=0, has_side_effects=True, vmem_limit_bytes=62 * 2**20
        ),
    )(fields, weight_one, weight_two, gate, shrink, *consts)
    return pl.pallas_call(
        unpack,
        name="unpack_rows",
        out_shape=jax.ShapeDtypeStruct((HL, WL, C), F32),
        in_specs=[any_spec],
        out_specs=any_spec,
        scratch_shapes=[vm((NG, NX, 3, WP, 128), F32), vm((HL, WL, C), F32), dma((NG, NX)), dma((NG, NX))],
        compiler_params=pltpu.CompilerParams(vmem_limit_bytes=60 * 2**20),
    )(packed)


def solution(mesh):
    in_specs = (
        P("lat", "lon", None),
        P(),
        P(),
        P(("lon", "lat"), None, None, None, None),
        P(("lon", "lat"), None, None, None, None),
    )
    out_specs = P("lat", "lon", None)
    return jax.shard_map(local, mesh=mesh, in_specs=in_specs, out_specs=out_specs, check_vma=False)
```

```python
import functools
import math

import jax
import jax.numpy as jnp
import ml_dtypes
import numpy as np
from jax import lax
from jax.experimental import pallas as pl
from jax.experimental.pallas import tpu as pltpu
from jax.sharding import PartitionSpec as P

MESH = pl.DeviceIdType.MESH
STEPS = (0, 1, 7, 2, 6, 3, 5, 4)
W = 720
H = 360
C = 96
KW = 256
NB = 8
NX = 4
NS = 32
HL = 45
WL = 180
WP = 184
KP = 192
RP = 12
NG = 3
MP = 384
NT = 9
MSG = NT * 8
MSG2 = 40
MSG1 = 24
F32 = jnp.float32
BF16 = jnp.bfloat16


def split_table(table):
    high = table.astype(ml_dtypes.bfloat16)
    low = (table - high.astype(np.float64)).astype(ml_dtypes.bfloat16)
    return np.stack([high, low])


@functools.lru_cache(None)
def tables():
    depth_z = np.arange(NB)[:, None, None]
    part = np.arange(2)[None, :, None]
    dest = np.arange(NS)[None, None, :]
    mode = 64 * (dest // 8) + 8 * depth_z + dest % 8 + 0 * part
    part = part + 0 * mode
    mode, part = mode.reshape(NB, 64), part.reshape(NB, 64)

    def wave(angle, which):
        return np.where(which == 0, np.cos(angle), -np.sin(angle))

    depth = np.arange(NX * KP)
    lon = 180 * (depth // KP) + depth % KP
    angle = 2 * math.pi / W * (mode[:, :, None] * lon % W)
    forward = wave(angle, part[:, :, None]) / math.sqrt(W) * (depth % KP < WL)

    rows = np.arange(NX * WP)
    lon = 180 * (rows // WP) + rows % WP
    angle = 2 * math.pi / W * (mode[:, None, :] * lon[:, None] % W)
    factor = np.where(mode == 0, 1.0, 2.0)[:, None, :]
    back = wave(angle, part[:, None, :]) * factor / math.sqrt(W) * (rows % WP < WL)[:, None]

    place = np.arange(MP)
    source = place % NS
    local_row = RP * (source // 8) + place // NS
    lat = HL * (source % 8) + local_row
    m = np.arange(MP)
    angle = 2 * math.pi / H * (m[:, None] * lat[None, :] % H)
    keep = (m < H)[:, None] * (local_row < HL)[None, :] / math.sqrt(H)
    cosine, sine = np.cos(angle) * keep, np.sin(angle) * keep
    lat_fwd = np.block([[cosine, sine], [-sine, cosine]])
    lat_back = lat_fwd.T
    order = (np.arange(NB)[:, None] + np.array(STEPS)[None, :]) % NB
    back = back[order].reshape(NB, 4, 2, NX * WP, 64).transpose(0, 1, 3, 2, 4).reshape(NB, 4, NX * WP, 128)
    return tuple(split_table(t) for t in (forward, lat_fwd, lat_back, back))


def high_low(value):
    high = value.astype(BF16)
    return high, (value - high.astype(F32)).astype(BF16)


def dot3(a, b, dims=((1,), (0,))):
    def one(p, q):
        return lax.dot_general(p, q, (dims, ((), ())), preferred_element_type=F32)

    return one(a[0], b[0]) + (one(a[0], b[1]) + one(a[1], b[0]))


NT_DIMS = ((1,), (1,))


def kernel(
    fields, w1, w2, gate, shrink, t_fwd, t_lat, t_bck, t_inv, out,
    fv, xs, xr, xhi, xlo, ys0, yr0, ys1, yr1,
    cs0, cr0, cs1, cr1, cs2, cr2, cs3, cr3, osn, gl, sl, gv, sv, wv, wt,
    vfwd, vlat, vbck, vinv, shi, slo, phi, plo, hhi, hlo, mhi, mlo,
    s_load, sf, sa, ra, sb, rb, sc, rc, sd, rd, sm, rm,
):
    x = lax.axis_index("lon")
    t = lax.axis_index("lat")
    z = t // 8
    yc = t % 8
    y = yc // 2
    core = yc % 2
    me = x * 8 + yc

    def field_copies(g):
        copies = []
        for s in range(NX):
            base = RP * s + 4 * g
            rows = pl.ds(base, min(4, HL - base))
            copies.append(pltpu.make_async_copy(fields.at[rows], fv.at[rows], sf.at[g, s]))
        return copies

    for copy in field_copies(0):
        copy.start()
    stages = [
        pltpu.make_async_copy(gate.at[0], gl, s_load.at[6]),
        pltpu.make_async_copy(shrink.at[0], sl, s_load.at[7]),
    ]
    for copy in stages:
        copy.start()
    for g in range(1, NG):
        for copy in field_copies(g):
            copy.start()
    loads = [
        pltpu.make_async_copy(w1.at[z], wv.at[0], s_load.at[0]),
        pltpu.make_async_copy(w2.at[z], wv.at[1], s_load.at[1]),
        pltpu.make_async_copy(t_fwd, vfwd, s_load.at[2]),
        pltpu.make_async_copy(t_lat, vlat, s_load.at[3]),
        pltpu.make_async_copy(t_bck, vbck, s_load.at[4]),
        pltpu.make_async_copy(t_inv.at[:, z], vinv, s_load.at[5]),
    ]
    def plane_peer(i):
        dx, r = lax.rem(i, 4), lax.div(i, 4)
        px = lax.rem(x + dx, 4)
        py = lax.rem(y + lax.div(r, 2) + dx, 4)
        pc = lax.rem(core + r + dx, 2)
        return px * 8 + py * 2 + pc

    def plane_id(d):
        return (lax.div(d, 8), z * 8 + lax.rem(d, 8))

    barrier = pltpu.get_barrier_semaphore()

    @pl.loop(1, NS)
    def _(i):
        d = plane_peer(i)
        pl.semaphore_signal(barrier, inc=1, device_id=plane_id(d), device_id_type=MESH)

    @pl.loop(1, NB)
    def _(i):
        pl.semaphore_signal(barrier, inc=1, device_id=(x, ((z + i) % 8) * 8 + yc), device_id_type=MESH)

    def pack(g, dx, put):
        base = RP * ((x + dx) % 4) + 4 * g
        last = fv[base + 3]
        for j in range(3):
            put(j, jnp.concatenate([fv[base + j], last[:, 32 * j : 32 * j + 32]], axis=1))

    def pack_group(g):
        for dx in (2, 1, 3):

            def put(j, value):
                xs[g, dx - 1, j, WP - 8 : WP] = jnp.zeros((8, 128), F32)
                xs[g, dx - 1, j, 0:WL] = value

            pack(g, dx, put)

    def send_group(g):
        for dx in (2, 1, 3):
            pltpu.make_async_remote_copy(
                src_ref=xs.at[g, dx - 1], dst_ref=xr.at[g, x], send_sem=sa.at[g], recv_sem=ra.at[g],
                device_id=((x + dx) % 4, t), device_id_type=MESH,
            ).start()

    def send_mask(src, dst, b, which):
        pltpu.make_async_remote_copy(
            src_ref=src.at[:, b], dst_ref=dst.at[z], send_sem=sm, recv_sem=rm.at[which],
            device_id=(x, b * 8 + yc), device_id_type=MESH,
        ).start()

    for copy in field_copies(0):
        copy.wait()
    pack_group(0)
    for copy in stages:
        copy.wait()
    pl.semaphore_wait(barrier, NS - 1 + NB - 1)
    for step, which in ((1, 0), (7, 0), (2, 0), (6, 1), (3, 1)):
        send_mask(gl, gv, (z + NB - step) % NB, which)
        send_mask(sl, sv, (z + NB - step) % NB, which)
    for step, which in ((5, 2), (4, 3)):
        send_mask(gl, gv, (z + NB - step) % NB, which)
        send_mask(sl, sv, (z + NB - step) % NB, which)
    send_group(0)
    pltpu.make_async_copy(gate.at[0, :, z], gv.at[z], rm.at[0]).start()
    pltpu.make_async_copy(shrink.at[0, :, z], sv.at[z], rm.at[0]).start()

    for copy in loads:
        copy.start()
    fv[HL : RP * NX] = jnp.zeros((RP * NX - HL, WL, C), F32)

    for g in range(1, NG):
        for copy in field_copies(g):
            copy.wait()
        pack_group(g)
        send_group(g)

    for g in range(NG):

        def put(j, value):
            xr[g, x, j, WP - 8 : WP] = jnp.zeros((8, 128), F32)
            xr[g, x, j, 0:WL] = value

        pack(g, 0, put)

    hhi[...] = jnp.zeros_like(hhi)
    hlo[...] = jnp.zeros_like(hlo)
    mhi[...] = jnp.zeros_like(mhi)
    mlo[...] = jnp.zeros_like(mlo)
    cs1[:, 36:MSG2, :] = jnp.zeros((NS, MSG2 - 36, 128), F32)
    for ref in (cs2, cs3):
        ref[:, 18:MSG1, :] = jnp.zeros((NS, MSG1 - 18, 128), F32)

    for copy in loads:
        copy.wait()
    turned_weights = []
    for which in range(2):
        wt[...] = jnp.zeros((256, 256), F32)
        wt[0:C, 0:C] = wv[which, 0]
        wt[0:C, 128 : 128 + C] = wv[which, 1]
        wt[128 : 128 + C, 0:C] = -wv[which, 1]
        wt[128 : 128 + C, 128 : 128 + C] = wv[which, 0]
        turned_weights.append(high_low(wt[...].T))

    def mode_at(u):
        return (z + STEPS[u]) % NB

    def send_plane(src, dst, send_sem, recv_sem, which):
        pltpu.make_async_copy(src.at[me], dst.at[me], recv_sem.at[which]).start()

        @pl.loop(1, NS)
        def _(i):
            d = plane_peer(i)
            pltpu.make_async_remote_copy(
                src_ref=src.at[d], dst_ref=dst.at[me], send_sem=send_sem.at[which], recv_sem=recv_sem.at[which],
                device_id=plane_id(d), device_id_type=MESH,
            ).start()

    ys0flat = ys0.reshape(NS * MSG, 128)
    ys1flat = ys1.reshape(NS * MSG, 128)
    ysflat = (ys0flat, ys1flat)
    for g in range(NG):
        pltpu.make_async_copy(xr.at[g, pl.ds(0, 3)], xr.at[g, pl.ds(0, 3)], ra.at[g]).wait()
        for s in range(NX):
            for j in range(3):
                value = jnp.concatenate([xr[g, s, j], jnp.zeros((KP - WP, 128), F32)], axis=0)
                high, low = high_low(value)
                xhi[KP * s : KP * s + KP, 128 * j : 128 * j + 128] = high
                xlo[KP * s : KP * s + KP, 128 * j : 128 * j + 128] = low
        for half in range(2):
            table = [jnp.concatenate([vfwd[k, mode_at(4 * half + u)] for u in range(4)], axis=0) for k in range(2)]
            modes = dot3(table, (xhi[...], xlo[...]))
            for u in range(4):
                for ri in range(2):
                    for j in range(3):
                        value = modes[64 * u + 32 * ri : 64 * u + 32 * ri + 32, 128 * j : 128 * j + 128]
                        row = 2 * (3 * g + j) + ri
                        ysflat[half][pl.ds(4 * row + u, NS, stride=MSG), :] = value
            if g == NG - 1 and half == 0:
                send_plane(ys0, yr0, sb, rb, 0)
            elif g == NG - 1:
                send_plane(ys1, yr1, sb, rb, 1)

    yr0flat = yr0.reshape(NS * MSG, 128)
    yr1flat = yr1.reshape(NS * MSG, 128)
    cs0flat = cs0.reshape(NS * MSG, 128)
    cs1flat = cs1.reshape(NS * MSG2, 128)
    cs2flat = cs2.reshape(NS * MSG1, 128)
    cs3flat = cs3.reshape(NS * MSG1, 128)
    cr0flat = cr0.reshape(NS * MSG, 128)
    cr1flat = cr1.reshape(NS * MSG2, 128)
    cr2flat = cr2.reshape(NS * MSG1, 128)
    cr3flat = cr3.reshape(NS * MSG1, 128)

    def strided(ref, units, pitch, unit):
        return lambda row: ref[pl.ds(units * row + unit, NS, stride=pitch), :]

    def lat_forward(sources):
        for pos, source in enumerate(sources):
            for ri in range(2):
                for g in range(NG):
                    tiles = [source(2 * (3 * g + j) + ri) for j in range(3)]
                    last = jnp.concatenate([v[:, C:] for v in tiles] + [tiles[0][:, C:]], axis=1)
                    for r, value in enumerate(tiles + [last]):
                        high, low = high_low(value)
                        at = ri * MP + (g * 4 + r) * NS
                        shi[at : at + NS, 128 * pos : 128 * pos + 128] = high
                        slo[at : at + NS, 128 * pos : 128 * pos + 128] = low
        spec = dot3((vlat[0], vlat[1]), (shi[...], slo[...]))
        for pos in range(2):
            for ri in range(2):
                high, low = high_low(spec[MP * ri : MP * ri + MP, 128 * pos : 128 * pos + 128])
                phi[pos, :, 128 * ri : 128 * ri + 128] = high
                plo[pos, :, 128 * ri : 128 * ri + 128] = low

    def lat_back(places, modes, put):
        first, second = turned_weights
        for pos, (place, q) in enumerate(zip(places, modes)):
            hid = dot3(first, (phi[place], plo[place]), NT_DIMS)
            for ri in range(2):
                high, low = high_low(hid[128 * ri : 128 * ri + C, 0:H] * gv[q, ri].astype(F32))
                hhi[128 * ri : 128 * ri + C, 0:H] = high
                hlo[128 * ri : 128 * ri + C, 0:H] = low
            mix = dot3(second, (hhi[...], hlo[...]))
            for ri in range(2):
                high, low = high_low(mix[128 * ri : 128 * ri + C, 0:H] * sv[q, ri].astype(F32))
                mhi[128 * pos : 128 * pos + C, MP * ri : MP * ri + H] = high
                mlo[128 * pos : 128 * pos + C, MP * ri : MP * ri + H] = low
        width = 128 * len(modes)
        band = dot3((vbck[0], vbck[1]), (mhi[0:width], mlo[0:width]), NT_DIMS)
        for pos in range(len(modes)):
            for ri in range(2):
                for g in range(NG):
                    at = ri * MP + g * 4 * NS
                    rows = [band[at + r * NS : at + r * NS + NS, 128 * pos : 128 * pos + 128] for r in range(4)]
                    for j in range(3):
                        value = jnp.concatenate([rows[j][:, 0:C], rows[3][:, 32 * j : 32 * j + 32]], axis=1)
                        put(2 * (3 * g + j) + ri, pos, value)

    def inverse_term(g, sources, slots):
        for u, source in enumerate(sources):
            for ri in range(2):
                for j in range(3):
                    high, low = high_low(source(2 * (3 * g + j) + ri))
                    at = 64 * u + 32 * ri
                    xhi[at : at + 32, 128 * j : 128 * j + 128] = high
                    xlo[at : at + 32, 128 * j : 128 * j + 128] = low
        table = [jnp.concatenate([vinv[k, i] for i in slots], axis=1) for k in range(2)]
        depth = 64 * len(sources)
        return dot3(table, (xhi[0:depth], xlo[0:depth]))

    def add_term(g, sources, slots, first=False):
        term = inverse_term(g, sources, slots)
        for s in range(NX):
            for j in range(3):
                value = term[WP * s : WP * s + WP, 128 * j : 128 * j + 128]
                osn[g, s, j] = value if first else osn[g, s, j] + value

    def arrived(ref, sem):
        pltpu.make_async_copy(ref, ref, sem).wait()

    arrived(yr0, rb.at[0])
    arrived(gv, rm.at[0])

    @pl.loop(0, 2)
    def _(slot):
        def put(row, pos, value):
            cs0flat[pl.ds(4 * row + 2 * slot + pos, NS, stride=MSG), :] = value

        lat_forward([strided(yr0flat, 4, MSG, 2 * slot + pos) for pos in range(2)])
        lat_back((0, 1), ((z + 7 * slot) % NB, (z + 1 + slot) % NB), put)

    send_plane(cs0, cr0, sc, rc, 0)

    arrived(yr1, rb.at[1])
    lat_forward([strided(yr1flat, 4, MSG, pos) for pos in range(2)])
    arrived(gv.at[pl.ds(0, 4)], rm.at[1])

    def put_next(row, pos, value):
        cs1flat[pl.ds(2 * row + pos, NS, stride=MSG2), :] = value

    lat_back((0, 1), (mode_at(4), mode_at(5)), put_next)
    send_plane(cs1, cr1, sc, rc, 1)

    lat_forward([strided(yr1flat, 4, MSG, 2 + pos) for pos in range(2)])
    arrived(cr0, rc.at[0])
    for g in range(NG):
        add_term(g, [strided(cr0flat, 4, MSG, u) for u in range(4)], (0, 1), first=True)

    def put_third(row, pos, value):
        cs2flat[pl.ds(row, NS, stride=MSG1), :] = value

    def put_last(row, pos, value):
        cs3flat[pl.ds(row, NS, stride=MSG1), :] = value

    arrived(gv.at[pl.ds(0, 2)], rm.at[2])
    lat_back((0,), (mode_at(6),), put_third)
    send_plane(cs2, cr2, sc, rc, 2)
    arrived(cr1, rc.at[1])
    for g in range(NG):
        add_term(g, [strided(cr1flat, 2, MSG2, u) for u in range(2)], (2,))
    arrived(gv.at[pl.ds(0, 2)], rm.at[3])
    lat_back((1,), (mode_at(7),), put_last)
    send_plane(cs3, cr3, sc, rc, 3)
    arrived(cr2, rc.at[2])
    arrived(cr3, rc.at[3])
    for g in range(NG):
        add_term(g, [strided(cr2flat, 1, MSG1, 0), strided(cr3flat, 1, MSG1, 0)], (3,))
        pltpu.make_async_copy(osn.at[g, x], out.at[g, x], rd.at[g]).start()
        for dx in (2, 1, 3):
            to = (x + dx) % 4
            pltpu.make_async_remote_copy(
                src_ref=osn.at[g, to], dst_ref=out.at[g, x], send_sem=sd.at[g], recv_sem=rd.at[g],
                device_id=(to, t), device_id_type=MESH,
            ).start()

    for g in range(NG):
        pltpu.make_async_copy(osn.at[g], osn.at[g], rd.at[g]).wait()
    for g in range(NG):
        pltpu.make_async_copy(xs.at[g], xs.at[g], sa.at[g]).wait()
        pltpu.make_async_copy(xs.at[g], xs.at[g], sd.at[g]).wait()
    for ref, sem in ((ys0, sb.at[0]), (ys1, sb.at[1]), (cs0, sc.at[0]), (cs1, sc.at[1]), (cs2, sc.at[2]), (cs3, sc.at[3])):
        arrived(ref.at[pl.ds(0, NS - 1)], sem)
    arrived(gv.at[pl.ds(0, 7)], sm)
    arrived(gv.at[pl.ds(0, 7)], sm)


def unpack(packed, out, tiles, rows, s_in, s_out):
    def load(g, s):
        return pltpu.make_async_copy(packed.at[g, s], tiles.at[g, s], s_in.at[g, s])

    def store(g, s):
        base = RP * s + 4 * g
        span = pl.ds(base, min(4, HL - base))
        return pltpu.make_async_copy(rows.at[span], out.at[span], s_out.at[g, s])

    order = [(g, s) for s in range(NX) for g in range(NG)]
    for g, s in order:
        load(g, s).start()
    for g, s in order:
        load(g, s).wait()
        base = RP * s + 4 * g
        count = min(4, HL - base)
        for r in range(min(3, count)):
            rows[base + r] = tiles[g, s, r, 0:WL, 0:C]
        if count == 4:
            rows[base + 3] = jnp.concatenate([tiles[g, s, r, 0:WL, C:] for r in range(3)], axis=1)
        store(g, s).start()
    for g, s in order:
        store(g, s).wait()


def local(fields, weight_one, weight_two, gate_mask, shrink_mask):
    gate = jnp.swapaxes(gate_mask, 3, 4)
    shrink = jnp.swapaxes(shrink_mask, 3, 4)
    consts = [jnp.asarray(t) for t in tables()]
    dma = pltpu.SemaphoreType.DMA
    any_spec = pl.BlockSpec(memory_space=pl.ANY)
    vm = pltpu.VMEM
    scratch = [
        vm((RP * NX, WL, C), F32),
        vm((NG, 3, 3, WP, 128), F32),
        vm((NG, NX, 3, WP, 128), F32),
        vm((NX * KP, 384), BF16),
        vm((NX * KP, 384), BF16),
        vm((NS, MSG, 128), F32),
        vm((NS, MSG, 128), F32),
        vm((NS, MSG, 128), F32),
        vm((NS, MSG, 128), F32),
        vm((NS, MSG, 128), F32),
        vm((NS, MSG, 128), F32),
        vm((NS, MSG2, 128), F32),
        vm((NS, MSG2, 128), F32),
        vm((NS, MSG1, 128), F32),
        vm((NS, MSG1, 128), F32),
        vm((NS, MSG1, 128), F32),
        vm((NS, MSG1, 128), F32),
        vm((NG, NX, 3, WP, 128), F32),
        vm((2, NB, C, H), jnp.int32),
        vm((2, NB, C, H), jnp.int32),
        vm((NB, 2, C, H), jnp.int32),
        vm((NB, 2, C, H), jnp.int32),
        vm((2, 2, C, C), F32),
        vm((256, 256), F32),
        vm((2, NB, 64, NX * KP), BF16),
        vm((2, 2 * MP, 2 * MP), BF16),
        vm((2, 2 * MP, 2 * MP), BF16),
        vm((2, 4, NX * WP, 128), BF16),
        vm((2 * MP, 256), BF16),
        vm((2 * MP, 256), BF16),
        vm((2, MP, 256), BF16),
        vm((2, MP, 256), BF16),
        vm((256, MP), BF16),
        vm((256, MP), BF16),
        vm((256, 2 * MP), BF16),
        vm((256, 2 * MP), BF16),
        dma((8,)),
        dma((NG, NX)),
        dma((NG,)),
        dma((NG,)),
        dma((2,)),
        dma((2,)),
        dma((4,)),
        dma((4,)),
        dma((NG,)),
        dma((NG,)),
        dma,
        dma((4,)),
    ]
    packed = pl.pallas_call(
        kernel,
        name="afno_tangent",
        out_shape=jax.ShapeDtypeStruct((NG, NX, 3, WP, 128), F32),
        in_specs=[any_spec] * 9,
        out_specs=any_spec,
        scratch_shapes=scratch,
        compiler_params=pltpu.CompilerParams(
            collective_id=0, has_side_effects=True, vmem_limit_bytes=62 * 2**20
        ),
    )(fields, weight_one, weight_two, gate, shrink, *consts)
    return pl.pallas_call(
        unpack,
        name="unpack_rows",
        out_shape=jax.ShapeDtypeStruct((HL, WL, C), F32),
        in_specs=[any_spec],
        out_specs=any_spec,
        scratch_shapes=[vm((NG, NX, 3, WP, 128), F32), vm((HL, WL, C), F32), dma((NG, NX)), dma((NG, NX))],
        compiler_params=pltpu.CompilerParams(vmem_limit_bytes=60 * 2**20),
    )(packed)


def solution(mesh):
    in_specs = (
        P("lat", "lon", None),
        P(),
        P(),
        P(("lon", "lat"), None, None, None, None),
        P(("lon", "lat"), None, None, None, None),
    )
    out_specs = P("lat", "lon", None)
    return jax.shard_map(local, mesh=mesh, in_specs=in_specs, out_specs=out_specs, check_vma=False)
```

```python
import functools
import math

import jax
import jax.numpy as jnp
import ml_dtypes
import numpy as np
from jax import lax
from jax.experimental import pallas as pl
from jax.experimental.pallas import tpu as pltpu
from jax.sharding import PartitionSpec as P

MESH = pl.DeviceIdType.MESH
STEPS = (0, 1, 7, 2, 6, 3, 5, 4)
W = 720
H = 360
C = 96
KW = 256
NB = 8
NX = 4
NS = 32
HL = 45
WL = 180
WP = 184
KP = 192
RP = 12
NG = 3
MP = 384
NT = 9
MSG = NT * 8
MSG2 = 40
MSG1 = 24
F32 = jnp.float32
BF16 = jnp.bfloat16


def split_table(table):
    high = table.astype(ml_dtypes.bfloat16)
    low = (table - high.astype(np.float64)).astype(ml_dtypes.bfloat16)
    return np.stack([high, low])


@functools.lru_cache(None)
def tables():
    depth_z = np.arange(NB)[:, None, None]
    part = np.arange(2)[None, :, None]
    dest = np.arange(NS)[None, None, :]
    mode = 64 * (dest // 8) + 8 * depth_z + dest % 8 + 0 * part
    part = part + 0 * mode
    mode, part = mode.reshape(NB, 64), part.reshape(NB, 64)

    def wave(angle, which):
        return np.where(which == 0, np.cos(angle), -np.sin(angle))

    depth = np.arange(NX * KP)
    lon = 180 * (depth // KP) + depth % KP
    angle = 2 * math.pi / W * (mode[:, :, None] * lon % W)
    forward = wave(angle, part[:, :, None]) / math.sqrt(W) * (depth % KP < WL)

    rows = np.arange(NX * WP)
    lon = 180 * (rows // WP) + rows % WP
    angle = 2 * math.pi / W * (mode[:, None, :] * lon[:, None] % W)
    factor = np.where(mode == 0, 1.0, 2.0)[:, None, :]
    back = wave(angle, part[:, None, :]) * factor / math.sqrt(W) * (rows % WP < WL)[:, None]

    place = np.arange(MP)
    source = place % NS
    local_row = RP * (source // 8) + place // NS
    lat = HL * (source % 8) + local_row
    m = np.arange(MP)
    angle = 2 * math.pi / H * (m[:, None] * lat[None, :] % H)
    keep = (m < H)[:, None] * (local_row < HL)[None, :] / math.sqrt(H)
    cosine, sine = np.cos(angle) * keep, np.sin(angle) * keep
    lat_fwd = np.block([[cosine, sine], [-sine, cosine]])
    lat_back = lat_fwd.T
    order = (np.arange(NB)[:, None] + np.array(STEPS)[None, :]) % NB
    back = back[order].reshape(NB, 4, 2, NX * WP, 64).transpose(0, 1, 3, 2, 4).reshape(NB, 4, NX * WP, 128)
    return tuple(split_table(t) for t in (forward, lat_fwd, lat_back, back))


def high_low(value):
    high = value.astype(BF16)
    return high, (value - high.astype(F32)).astype(BF16)


def dot3(a, b, dims=((1,), (0,))):
    def one(p, q):
        return lax.dot_general(p, q, (dims, ((), ())), preferred_element_type=F32)

    return one(a[0], b[0]) + (one(a[0], b[1]) + one(a[1], b[0]))


NT_DIMS = ((1,), (1,))


def kernel(
    fields, w1, w2, gate, shrink, t_fwd, t_lat, t_bck, t_inv, out,
    fv, xs, xr, xhi, xlo, ys0, yr0, ys1, yr1,
    cs0, cr0, cs1, cr1, cs2, cr2, cs3, cr3, osn, gl, sl, gv, sv, wv, wt,
    vfwd, vlat, vbck, vinv, shi, slo, phi, plo, hhi, hlo, mhi, mlo,
    s_load, sf, sa, ra, sb, rb, sc, rc, sd, rd, sm, rm,
):
    x = lax.axis_index("lon")
    t = lax.axis_index("lat")
    z = t // 8
    yc = t % 8
    y = yc // 2
    core = yc % 2
    me = x * 8 + yc

    def field_copies(g):
        copies = []
        for s in range(NX):
            base = RP * s + 4 * g
            rows = pl.ds(base, min(4, HL - base))
            copies.append(pltpu.make_async_copy(fields.at[rows], fv.at[rows], sf.at[g, s]))
        return copies

    for copy in field_copies(0):
        copy.start()
    stages = [
        pltpu.make_async_copy(gate.at[0], gl, s_load.at[6]),
        pltpu.make_async_copy(shrink.at[0], sl, s_load.at[7]),
    ]
    for copy in stages:
        copy.start()
    for g in range(1, NG):
        for copy in field_copies(g):
            copy.start()
    loads = [
        pltpu.make_async_copy(w1.at[z], wv.at[0], s_load.at[0]),
        pltpu.make_async_copy(w2.at[z], wv.at[1], s_load.at[1]),
        pltpu.make_async_copy(t_fwd, vfwd, s_load.at[2]),
        pltpu.make_async_copy(t_lat, vlat, s_load.at[3]),
        pltpu.make_async_copy(t_bck, vbck, s_load.at[4]),
        pltpu.make_async_copy(t_inv.at[:, z], vinv, s_load.at[5]),
    ]
    def plane_peer(i):
        dx, r = lax.rem(i, 4), lax.div(i, 4)
        px = lax.rem(x + dx, 4)
        py = lax.rem(y + lax.div(r, 2) + dx, 4)
        pc = lax.rem(core + r + dx, 2)
        return px * 8 + py * 2 + pc

    def plane_id(d):
        return (lax.div(d, 8), z * 8 + lax.rem(d, 8))

    barrier = pltpu.get_barrier_semaphore()

    @pl.loop(1, NS)
    def _(i):
        d = plane_peer(i)
        pl.semaphore_signal(barrier, inc=1, device_id=plane_id(d), device_id_type=MESH)

    @pl.loop(1, NB)
    def _(i):
        pl.semaphore_signal(barrier, inc=1, device_id=(x, ((z + i) % 8) * 8 + yc), device_id_type=MESH)

    def pack(g, dx, put):
        base = RP * ((x + dx) % 4) + 4 * g
        last = fv[base + 3]
        for j in range(3):
            put(j, jnp.concatenate([fv[base + j], last[:, 32 * j : 32 * j + 32]], axis=1))

    def pack_group(g):
        for dx in (2, 1, 3):

            def put(j, value):
                xs[g, dx - 1, j, WP - 8 : WP] = jnp.zeros((8, 128), F32)
                xs[g, dx - 1, j, 0:WL] = value

            pack(g, dx, put)

    def send_group(g):
        for dx in (2, 1, 3):
            pltpu.make_async_remote_copy(
                src_ref=xs.at[g, dx - 1], dst_ref=xr.at[g, x], send_sem=sa.at[g], recv_sem=ra.at[g],
                device_id=((x + dx) % 4, t), device_id_type=MESH,
            ).start()

    def send_mask(src, dst, b, which):
        pltpu.make_async_remote_copy(
            src_ref=src.at[:, b], dst_ref=dst.at[z], send_sem=sm, recv_sem=rm.at[which],
            device_id=(x, b * 8 + yc), device_id_type=MESH,
        ).start()

    for copy in field_copies(0):
        copy.wait()
    pack_group(0)
    for copy in stages:
        copy.wait()
    pl.semaphore_wait(barrier, NS - 1 + NB - 1)
    for step, which in ((1, 0), (7, 0), (2, 0), (6, 1), (3, 1)):
        send_mask(gl, gv, (z + NB - step) % NB, which)
        send_mask(sl, sv, (z + NB - step) % NB, which)
    for step, which in ((5, 2), (4, 3)):
        send_mask(gl, gv, (z + NB - step) % NB, which)
        send_mask(sl, sv, (z + NB - step) % NB, which)
    send_group(0)
    pltpu.make_async_copy(gate.at[0, :, z], gv.at[z], rm.at[0]).start()
    pltpu.make_async_copy(shrink.at[0, :, z], sv.at[z], rm.at[0]).start()

    for copy in loads:
        copy.start()
    fv[HL : RP * NX] = jnp.zeros((RP * NX - HL, WL, C), F32)

    for g in range(1, NG):
        for copy in field_copies(g):
            copy.wait()
        pack_group(g)
        send_group(g)

    for g in range(NG):

        def put(j, value):
            xr[g, x, j, WP - 8 : WP] = jnp.zeros((8, 128), F32)
            xr[g, x, j, 0:WL] = value

        pack(g, 0, put)

    hhi[...] = jnp.zeros_like(hhi)
    hlo[...] = jnp.zeros_like(hlo)
    mhi[...] = jnp.zeros_like(mhi)
    mlo[...] = jnp.zeros_like(mlo)
    cs1[:, 36:MSG2, :] = jnp.zeros((NS, MSG2 - 36, 128), F32)
    for ref in (cs2, cs3):
        ref[:, 18:MSG1, :] = jnp.zeros((NS, MSG1 - 18, 128), F32)

    for copy in loads:
        copy.wait()
    turned_weights = []
    for which in range(2):
        wt[...] = jnp.zeros((256, 256), F32)
        wt[0:C, 0:C] = wv[which, 0]
        wt[0:C, 128 : 128 + C] = wv[which, 1]
        wt[128 : 128 + C, 0:C] = -wv[which, 1]
        wt[128 : 128 + C, 128 : 128 + C] = wv[which, 0]
        turned_weights.append(high_low(wt[...].T))

    def mode_at(u):
        return (z + STEPS[u]) % NB

    def send_plane(src, dst, send_sem, recv_sem, which):
        pltpu.make_async_copy(src.at[me], dst.at[me], recv_sem.at[which]).start()

        @pl.loop(1, NS)
        def _(i):
            d = plane_peer(i)
            pltpu.make_async_remote_copy(
                src_ref=src.at[d], dst_ref=dst.at[me], send_sem=send_sem.at[which], recv_sem=recv_sem.at[which],
                device_id=plane_id(d), device_id_type=MESH,
            ).start()

    ys0flat = ys0.reshape(NS * MSG, 128)
    ys1flat = ys1.reshape(NS * MSG, 128)
    ysflat = (ys0flat, ys1flat)
    for g in range(NG):
        pltpu.make_async_copy(xr.at[g, pl.ds(0, 3)], xr.at[g, pl.ds(0, 3)], ra.at[g]).wait()
        for s in range(NX):
            for j in range(3):
                value = jnp.concatenate([xr[g, s, j], jnp.zeros((KP - WP, 128), F32)], axis=0)
                high, low = high_low(value)
                xhi[KP * s : KP * s + KP, 128 * j : 128 * j + 128] = high
                xlo[KP * s : KP * s + KP, 128 * j : 128 * j + 128] = low
        for half in range(2):
            table = [jnp.concatenate([vfwd[k, mode_at(4 * half + u)] for u in range(4)], axis=0) for k in range(2)]
            modes = dot3(table, (xhi[...], xlo[...]))
            for u in range(4):
                for ri in range(2):
                    for j in range(3):
                        value = modes[64 * u + 32 * ri : 64 * u + 32 * ri + 32, 128 * j : 128 * j + 128]
                        row = 2 * (3 * g + j) + ri
                        ysflat[half][pl.ds(4 * row + u, NS, stride=MSG), :] = value
            if g == NG - 1 and half == 0:
                send_plane(ys0, yr0, sb, rb, 0)
            elif g == NG - 1:
                send_plane(ys1, yr1, sb, rb, 1)

    yr0flat = yr0.reshape(NS * MSG, 128)
    yr1flat = yr1.reshape(NS * MSG, 128)
    cs0flat = cs0.reshape(NS * MSG, 128)
    cs1flat = cs1.reshape(NS * MSG2, 128)
    cs2flat = cs2.reshape(NS * MSG1, 128)
    cs3flat = cs3.reshape(NS * MSG1, 128)
    cr0flat = cr0.reshape(NS * MSG, 128)
    cr1flat = cr1.reshape(NS * MSG2, 128)
    cr2flat = cr2.reshape(NS * MSG1, 128)
    cr3flat = cr3.reshape(NS * MSG1, 128)

    def strided(ref, units, pitch, unit):
        return lambda row: ref[pl.ds(units * row + unit, NS, stride=pitch), :]

    def lat_forward(sources):
        for pos, source in enumerate(sources):
            for ri in range(2):
                for g in range(NG):
                    tiles = [source(2 * (3 * g + j) + ri) for j in range(3)]
                    last = jnp.concatenate([v[:, C:] for v in tiles] + [tiles[0][:, C:]], axis=1)
                    for r, value in enumerate(tiles + [last]):
                        high, low = high_low(value)
                        at = ri * MP + (g * 4 + r) * NS
                        shi[at : at + NS, 128 * pos : 128 * pos + 128] = high
                        slo[at : at + NS, 128 * pos : 128 * pos + 128] = low
        spec = dot3((vlat[0], vlat[1]), (shi[...], slo[...]))
        for pos in range(2):
            for ri in range(2):
                high, low = high_low(spec[MP * ri : MP * ri + MP, 128 * pos : 128 * pos + 128])
                phi[pos, :, 128 * ri : 128 * ri + 128] = high
                plo[pos, :, 128 * ri : 128 * ri + 128] = low

    def lat_back(places, modes, put):
        first, second = turned_weights
        for pos, (place, q) in enumerate(zip(places, modes)):
            hid = dot3(first, (phi[place], plo[place]), NT_DIMS)
            for ri in range(2):
                high, low = high_low(hid[128 * ri : 128 * ri + C, 0:H] * gv[q, ri].astype(F32))
                hhi[128 * ri : 128 * ri + C, 0:H] = high
                hlo[128 * ri : 128 * ri + C, 0:H] = low
            mix = dot3(second, (hhi[...], hlo[...]))
            for ri in range(2):
                high, low = high_low(mix[128 * ri : 128 * ri + C, 0:H] * sv[q, ri].astype(F32))
                mhi[128 * pos : 128 * pos + C, MP * ri : MP * ri + H] = high
                mlo[128 * pos : 128 * pos + C, MP * ri : MP * ri + H] = low
        width = 128 * len(modes)
        band = dot3((vbck[0], vbck[1]), (mhi[0:width], mlo[0:width]), NT_DIMS)
        for pos in range(len(modes)):
            for ri in range(2):
                for g in range(NG):
                    at = ri * MP + g * 4 * NS
                    rows = [band[at + r * NS : at + r * NS + NS, 128 * pos : 128 * pos + 128] for r in range(4)]
                    for j in range(3):
                        value = jnp.concatenate([rows[j][:, 0:C], rows[3][:, 32 * j : 32 * j + 32]], axis=1)
                        put(2 * (3 * g + j) + ri, pos, value)

    def inverse_term(g, sources, slots):
        for u, source in enumerate(sources):
            for ri in range(2):
                for j in range(3):
                    high, low = high_low(source(2 * (3 * g + j) + ri))
                    at = 64 * u + 32 * ri
                    xhi[at : at + 32, 128 * j : 128 * j + 128] = high
                    xlo[at : at + 32, 128 * j : 128 * j + 128] = low
        table = [jnp.concatenate([vinv[k, i] for i in slots], axis=1) for k in range(2)]
        depth = 64 * len(sources)
        return dot3(table, (xhi[0:depth], xlo[0:depth]))

    def add_term(g, sources, slots, first=False):
        term = inverse_term(g, sources, slots)
        for s in range(NX):
            for j in range(3):
                value = term[WP * s : WP * s + WP, 128 * j : 128 * j + 128]
                osn[g, s, j] = value if first else osn[g, s, j] + value

    def arrived(ref, sem):
        pltpu.make_async_copy(ref, ref, sem).wait()

    arrived(yr0, rb.at[0])
    arrived(gv, rm.at[0])

    @pl.loop(0, 2)
    def _(slot):
        def put(row, pos, value):
            cs0flat[pl.ds(4 * row + 2 * slot + pos, NS, stride=MSG), :] = value

        lat_forward([strided(yr0flat, 4, MSG, 2 * slot + pos) for pos in range(2)])
        lat_back((0, 1), ((z + 7 * slot) % NB, (z + 1 + slot) % NB), put)

    send_plane(cs0, cr0, sc, rc, 0)

    arrived(yr1, rb.at[1])
    lat_forward([strided(yr1flat, 4, MSG, pos) for pos in range(2)])
    arrived(gv.at[pl.ds(0, 4)], rm.at[1])

    def put_next(row, pos, value):
        cs1flat[pl.ds(2 * row + pos, NS, stride=MSG2), :] = value

    lat_back((0, 1), (mode_at(4), mode_at(5)), put_next)
    send_plane(cs1, cr1, sc, rc, 1)

    lat_forward([strided(yr1flat, 4, MSG, 2 + pos) for pos in range(2)])

    def put_third(row, pos, value):
        cs2flat[pl.ds(row, NS, stride=MSG1), :] = value

    def put_last(row, pos, value):
        cs3flat[pl.ds(row, NS, stride=MSG1), :] = value

    arrived(gv.at[pl.ds(0, 2)], rm.at[2])
    lat_back((0,), (mode_at(6),), put_third)
    send_plane(cs2, cr2, sc, rc, 2)
    arrived(gv.at[pl.ds(0, 2)], rm.at[3])
    lat_back((1,), (mode_at(7),), put_last)
    send_plane(cs3, cr3, sc, rc, 3)
    arrived(cr0, rc.at[0])
    for g in range(NG):
        add_term(g, [strided(cr0flat, 4, MSG, u) for u in range(4)], (0, 1), first=True)
    arrived(cr1, rc.at[1])
    for g in range(NG):
        add_term(g, [strided(cr1flat, 2, MSG2, u) for u in range(2)], (2,))
    arrived(cr2, rc.at[2])
    arrived(cr3, rc.at[3])
    for g in range(NG):
        add_term(g, [strided(cr2flat, 1, MSG1, 0), strided(cr3flat, 1, MSG1, 0)], (3,))
        pltpu.make_async_copy(osn.at[g, x], out.at[g, x], rd.at[g]).start()
        for dx in (2, 1, 3):
            to = (x + dx) % 4
            pltpu.make_async_remote_copy(
                src_ref=osn.at[g, to], dst_ref=out.at[g, x], send_sem=sd.at[g], recv_sem=rd.at[g],
                device_id=(to, t), device_id_type=MESH,
            ).start()

    for g in range(NG):
        pltpu.make_async_copy(osn.at[g], osn.at[g], rd.at[g]).wait()
    for g in range(NG):
        pltpu.make_async_copy(xs.at[g], xs.at[g], sa.at[g]).wait()
        pltpu.make_async_copy(xs.at[g], xs.at[g], sd.at[g]).wait()
    for ref, sem in ((ys0, sb.at[0]), (ys1, sb.at[1]), (cs0, sc.at[0]), (cs1, sc.at[1]), (cs2, sc.at[2]), (cs3, sc.at[3])):
        arrived(ref.at[pl.ds(0, NS - 1)], sem)
    arrived(gv.at[pl.ds(0, 7)], sm)
    arrived(gv.at[pl.ds(0, 7)], sm)


def unpack(packed, out, tiles, rows, s_in, s_out):
    def load(g, s):
        return pltpu.make_async_copy(packed.at[g, s], tiles.at[g, s], s_in.at[g, s])

    def store(g, s):
        base = RP * s + 4 * g
        span = pl.ds(base, min(4, HL - base))
        return pltpu.make_async_copy(rows.at[span], out.at[span], s_out.at[g, s])

    order = [(g, s) for s in range(NX) for g in range(NG)]
    for g, s in order:
        load(g, s).start()
    for g, s in order:
        load(g, s).wait()
        base = RP * s + 4 * g
        count = min(4, HL - base)
        for r in range(min(3, count)):
            rows[base + r] = tiles[g, s, r, 0:WL, 0:C]
        if count == 4:
            rows[base + 3] = jnp.concatenate([tiles[g, s, r, 0:WL, C:] for r in range(3)], axis=1)
        store(g, s).start()
    for g, s in order:
        store(g, s).wait()


def local(fields, weight_one, weight_two, gate_mask, shrink_mask):
    gate = jnp.swapaxes(gate_mask, 3, 4)
    shrink = jnp.swapaxes(shrink_mask, 3, 4)
    consts = [jnp.asarray(t) for t in tables()]
    dma = pltpu.SemaphoreType.DMA
    any_spec = pl.BlockSpec(memory_space=pl.ANY)
    vm = pltpu.VMEM
    scratch = [
        vm((RP * NX, WL, C), F32),
        vm((NG, 3, 3, WP, 128), F32),
        vm((NG, NX, 3, WP, 128), F32),
        vm((NX * KP, 384), BF16),
        vm((NX * KP, 384), BF16),
        vm((NS, MSG, 128), F32),
        vm((NS, MSG, 128), F32),
        vm((NS, MSG, 128), F32),
        vm((NS, MSG, 128), F32),
        vm((NS, MSG, 128), F32),
        vm((NS, MSG, 128), F32),
        vm((NS, MSG2, 128), F32),
        vm((NS, MSG2, 128), F32),
        vm((NS, MSG1, 128), F32),
        vm((NS, MSG1, 128), F32),
        vm((NS, MSG1, 128), F32),
        vm((NS, MSG1, 128), F32),
        vm((NG, NX, 3, WP, 128), F32),
        vm((2, NB, C, H), jnp.int32),
        vm((2, NB, C, H), jnp.int32),
        vm((NB, 2, C, H), jnp.int32),
        vm((NB, 2, C, H), jnp.int32),
        vm((2, 2, C, C), F32),
        vm((256, 256), F32),
        vm((2, NB, 64, NX * KP), BF16),
        vm((2, 2 * MP, 2 * MP), BF16),
        vm((2, 2 * MP, 2 * MP), BF16),
        vm((2, 4, NX * WP, 128), BF16),
        vm((2 * MP, 256), BF16),
        vm((2 * MP, 256), BF16),
        vm((2, MP, 256), BF16),
        vm((2, MP, 256), BF16),
        vm((256, MP), BF16),
        vm((256, MP), BF16),
        vm((256, 2 * MP), BF16),
        vm((256, 2 * MP), BF16),
        dma((8,)),
        dma((NG, NX)),
        dma((NG,)),
        dma((NG,)),
        dma((2,)),
        dma((2,)),
        dma((4,)),
        dma((4,)),
        dma((NG,)),
        dma((NG,)),
        dma,
        dma((4,)),
    ]
    packed = pl.pallas_call(
        kernel,
        name="afno_tangent",
        out_shape=jax.ShapeDtypeStruct((NG, NX, 3, WP, 128), F32),
        in_specs=[any_spec] * 9,
        out_specs=any_spec,
        scratch_shapes=scratch,
        compiler_params=pltpu.CompilerParams(
            collective_id=0, has_side_effects=True, vmem_limit_bytes=62 * 2**20
        ),
    )(fields, weight_one, weight_two, gate, shrink, *consts)
    return pl.pallas_call(
        unpack,
        name="unpack_rows",
        out_shape=jax.ShapeDtypeStruct((HL, WL, C), F32),
        in_specs=[any_spec],
        out_specs=any_spec,
        scratch_shapes=[vm((NG, NX, 3, WP, 128), F32), vm((HL, WL, C), F32), dma((NG, NX)), dma((NG, NX))],
        compiler_params=pltpu.CompilerParams(vmem_limit_bytes=60 * 2**20),
    )(packed)


def solution(mesh):
    in_specs = (
        P("lat", "lon", None),
        P(),
        P(),
        P(("lon", "lat"), None, None, None, None),
        P(("lon", "lat"), None, None, None, None),
    )
    out_specs = P("lat", "lon", None)
    return jax.shard_map(local, mesh=mesh, in_specs=in_specs, out_specs=out_specs, check_vma=False)
```
